256 devices in a mesh: dp: 16 (over y_hi, x, core), mp: 16 (over y_lo, z).
Axes of the slice: x: 4, y: 4 (y_hi: 2, y_lo: 2; y = y_hi * 2 + y_lo), z: 8, core: 2. Of those that a mesh axis runs over, the one named last changes fastest.
Arguments:
- tokens: bfloat16 [4096, 6144], P('dp'), may hold values from -6 to 6
- norm_gain: float32 [6144], replicated, may hold values from 0.1 to 1.9
- head_gains: float32 [2, 4096], P(None, 'mp'), may hold values from 0.5 to 12
- w_heads: bfloat16 [6144, 3, 4096], P('dp', None, 'mp'), may hold values from -0.078125 to 0.078125
- w_merge: bfloat16 [4096, 6144], P('mp'), may hold values from -0.5 to 0.5
- w_up: bfloat16 [6144, 12288], P('dp', 'mp'), may hold values from -0.078125 to 0.078125
- w_down: bfloat16 [12288, 6144], P('mp', 'dp'), may hold values from -0.0546875 to 0.0546875
- feed_in: bfloat16 [48, 128, 128], replicated, may hold values from -2 to 2
- feed_merge: bfloat16 [32, 128, 128], P('mp'), may hold values from -2 to 2
- feed_down: bfloat16 [96, 128, 128], P('mp'), may hold values from -2 to 2
- layer_bits: int32 [4], replicated, may hold values from 2 to 4
- hidden_keep: int32 [96], P('mp'), may hold values from 0 to 1, as said below
Outputs:
- branch: bfloat16 [4096, 6144], P('dp', 'mp')
- gram_in: float32 [48, 128, 128], P('mp')
- gram_hidden: float32 [96, 128, 128], P('mp')
The draws below stay inside these ranges and needn't reach their ends.
Inputs may be any that keep to these rules, and one draw needn't show every extreme that they name: `hidden_keep`: 1 keeps and 0 drops a group of 128 hidden units.
All inputs are finite; a program needn't handle non-finite values.
Results may differ from the reference program's by a relative error of at most 0.02.
The reference program's roundings to bfloat16 on the way count: a program that leaves them out, or rounds other values in their place, can miss the bound.
Values may be sent and summed in bfloat16 or wider, within the bound.
No kernel may reach another device: no remote copies, remote signals or barrier semaphores. Data moves between devices by JAX's collectives and lax.ppermute only.
A program may use at most 256 MiB of HBM per device.

```python
import math
import jax
import jax.numpy as jnp
from jax import lax

D = 6144
HD = 128
HEADS_DEV = 2
FF_DEV = 768
BLK = 128
PATCHES = 256
TOKENS = 4096
HEADS = 32
FF = 12288
N_MP = 16


def draw_head_gains(key, part):
    key = jax.random.fold_in(key, 11)
    second_key = jax.random.fold_in(key, 1)
    spread = jax.random.uniform(second_key, (2, HEADS, HD), jnp.float32, math.log(0.5), math.log(2.0))
    gains = jnp.exp(spread)
    return gains.reshape(2, HEADS * HD).astype(jnp.float32)


def draw_hidden_keep(key, part):
    key = jax.random.fold_in(key, 23)
    quota_key, rank_key = jax.random.split(key)
    per_device = FF_DEV // BLK
    device_count = FF // FF_DEV
    quota = jax.random.randint(quota_key, (device_count, 1), 1, per_device + 1)
    ranks = jax.random.randint(rank_key, (device_count, per_device), 0, per_device)
    return (ranks < quota).astype(jnp.int32).reshape(device_count * per_device)


def with_ends(drawn, rng, least, top_value):
    place = [jax.random.randint(jax.random.fold_in(rng, axis), (), 0, length) for axis, length in enumerate(drawn.shape)]
    longest = drawn.shape.index(max(drawn.shape))
    next_to = place[:longest] + [(place[longest] + 1) % drawn.shape[longest]] + place[longest + 1:]
    return drawn.at[tuple(place)].set(least).at[tuple(next_to)].set(top_value)


def steps_of(rng, extent, cuts, low, largest):
    gain = 1.0
    for dim, shards_of in cuts:
        draws = jax.random.uniform(jax.random.fold_in(jax.random.fold_in(rng, 6), dim), (shards_of,), jnp.float32, low / len(cuts), largest / len(cuts))
        gain = gain * jnp.repeat(jnp.exp(draws), extent[dim] // shards_of).reshape((-1,) + (1,) * (len(extent) - 1 - dim))
    return gain


def noise(key, shape, deviation, bound, shards=(), kind=jnp.bfloat16):
    gain = steps_of(key, shape, shards, -0.22, 0.18) if shards else 1.0
    values = jax.random.normal(key, shape, jnp.float32) * deviation * gain
    return jnp.minimum(jnp.maximum(values, -bound), bound).astype(kind)


def setup_inputs(seed: int = 0) -> dict:
    key_list = jax.random.split(jax.random.key(seed), 13)
    return {
        "tokens": noise(key_list[0], (TOKENS, D), 1.0, 6.0, ((0, 16),)),
        "norm_gain": jnp.clip(1.0 + 0.18 * jax.random.normal(key_list[1], (D,), jnp.float32), 0.1, 1.9),
        "head_gains": draw_head_gains(jax.random.fold_in(key_list[12], 71), 0),
        "w_heads": noise(key_list[3], (D, 3, HEADS * HD), D ** -0.5, 0.078125, ((0, 16), (2, 16))),
        "w_merge": noise(key_list[4], (HEADS * HD, D), HD ** -0.5, 0.5, ((0, 16),)),
        "w_up": noise(key_list[5], (D, FF), D ** -0.5, 0.078125, ((0, 16), (1, 16))),
        "w_down": noise(key_list[6], (FF, D), FF ** -0.5, 0.0546875, ((0, 16), (1, 16))),
        "feed_in": noise(key_list[7], (D // BLK, BLK, BLK), 0.15, 2.0),
        "feed_merge": noise(key_list[8], (HEADS * HD // BLK, BLK, BLK), 0.15, 2.0, ((0, 16),)),
        "feed_down": noise(key_list[9], (FF // BLK, BLK, BLK), 0.15, 2.0, ((0, 16),)),
        "layer_bits": with_ends(jax.random.randint(key_list[10], (4,), 2, 5), jax.random.fold_in(key_list[10], 1), 2, 4).astype(jnp.int32),
        "hidden_keep": draw_hidden_keep(jax.random.fold_in(key_list[12], 71), 0),
    }


def normalize(values, gain_row):
    row_mean = lax.optimization_barrier(jnp.mean(values, axis=-1, keepdims=True))
    centred = values - row_mean
    variance = lax.optimization_barrier(jnp.mean(centred * centred, axis=-1, keepdims=True))
    return centred * lax.rsqrt(variance + 1e-06) * gain_row

def soft_round(values, step_size):
    angle_arg = 2.0 * math.pi * values / step_size
    return values - step_size * jnp.sin(angle_arg) / (2.0 * math.pi)

def column_peak(weight):
    return lax.optimization_barrier(jnp.max(jnp.abs(weight.astype(jnp.float32)), axis=0))

def quantize(weight, feed_blocks, col_peak, bit_count):
    levels = jnp.exp2(bit_count.astype(jnp.float32) - 1.0) - 1.0
    step_size = (col_peak + 1e-06) / levels
    whole_f = weight.astype(jnp.float32)
    residual = (whole_f - soft_round(whole_f, step_size)).astype(jnp.bfloat16)
    blocks = residual.reshape(feed_blocks.shape[0], feed_blocks.shape[1], -1)
    correction = jnp.einsum('kij,kjc->kic', feed_blocks.astype(jnp.float32), blocks.astype(jnp.float32))
    adjusted = whole_f - correction.reshape(whole_f.shape)
    return soft_round(adjusted, step_size).astype(jnp.bfloat16)

def attend_image(triple):
    query_img, key_img, value_img = triple
    scores = jnp.einsum('qhd,khd->hqk', query_img.astype(jnp.float32), key_img.astype(jnp.float32)) / math.sqrt(HD)
    weights = jax.nn.softmax(scores, axis=-1).astype(jnp.bfloat16)
    mixed = jnp.einsum('hqk,khd->qhd', weights.astype(jnp.float32), value_img.astype(jnp.float32))
    return mixed.astype(jnp.bfloat16)

def reference(tokens, norm_gain, head_gains, w_heads, w_merge, w_up, w_down, feed_in, feed_merge, feed_down, layer_bits, hidden_keep):
    normed = normalize(tokens.astype(jnp.float32), norm_gain).astype(jnp.bfloat16)
    flat_heads = w_heads.reshape(D, -1)
    q_heads = quantize(flat_heads, feed_in, column_peak(flat_heads), layer_bits[0])
    q_merge = quantize(w_merge, feed_merge, column_peak(w_merge), layer_bits[1])
    q_up = quantize(w_up, feed_in, column_peak(w_up), layer_bits[2])
    q_down = quantize(w_down, feed_down, column_peak(w_down), layer_bits[3])
    projected = jnp.dot(normed, q_heads, preferred_element_type=jnp.float32).reshape(TOKENS, 3, HEADS, HD)
    gain_pair = head_gains.reshape(2, HEADS, HD)
    query = normalize(projected[:, 0], gain_pair[0]).astype(jnp.bfloat16)
    keyed = normalize(projected[:, 1], gain_pair[1]).astype(jnp.bfloat16)
    value = projected[:, 2].astype(jnp.bfloat16)
    image_count = TOKENS // PATCHES
    shaped = (query.reshape(image_count, PATCHES, HEADS, HD), keyed.reshape(image_count, PATCHES, HEADS, HD), value.reshape(image_count, PATCHES, HEADS, HD))
    attended = lax.map(attend_image, shaped).reshape(TOKENS, HEADS * HD)
    keep_cols = jnp.broadcast_to(hidden_keep[:, None], (FF // BLK, BLK)).reshape(FF).astype(jnp.float32)
    up_sum = jnp.dot(normed, q_up, preferred_element_type=jnp.float32)
    hidden = (jax.nn.gelu(up_sum, approximate=False) * keep_cols).astype(jnp.bfloat16)
    attn_groups = attended.reshape(TOKENS, N_MP, HEADS_DEV * HD).transpose(1, 0, 2)
    merge_groups = q_merge.reshape(N_MP, HEADS_DEV * HD, D)
    hidden_groups = hidden.reshape(TOKENS, N_MP, FF_DEV).transpose(1, 0, 2)
    down_groups = q_down.reshape(N_MP, FF_DEV, D)

    def add_group(running, group_items):
        attn_piece, merge_piece, hidden_piece, down_piece = group_items
        partial_sum = jnp.dot(attn_piece, merge_piece, preferred_element_type=jnp.float32)
        partial_sum = partial_sum + jnp.dot(hidden_piece, down_piece, preferred_element_type=jnp.float32)
        rounded = lax.optimization_barrier(partial_sum.astype(jnp.bfloat16))
        return (running + rounded.astype(jnp.float32), None)
    initial = jnp.zeros((TOKENS, D), jnp.float32)
    summed, unused = lax.scan(add_group, initial, (attn_groups, merge_groups, hidden_groups, down_groups))
    branch = summed.astype(jnp.bfloat16)
    normed_blocks = normed.reshape(TOKENS, D // BLK, BLK).astype(jnp.float32)
    gram_in = jnp.einsum('tbi,tbj->bij', normed_blocks, normed_blocks) / TOKENS
    hidden_blocks = hidden.reshape(TOKENS, FF // BLK, BLK).astype(jnp.float32)
    gram_hidden = jnp.einsum('tbi,tbj->bij', hidden_blocks, hidden_blocks) / TOKENS
    return (branch, gram_in, gram_hidden)
```

```python
import math

import jax
import jax.numpy as jnp
from jax import lax
from jax.experimental import pallas as pl
from jax.experimental.pallas import tpu as pltpu
from jax.sharding import PartitionSpec as P

HD = 128
BLK = 128
SINE = (25.13273048400879, -64.83467864990234, 67.04389953613281, -38.12319564819336, 12.233301162719727)
SPAN = 384
COST = pl.CostEstimate(flops=0, bytes_accessed=0, transcendentals=0)
VMEM_LIMIT = 28 * 2**20
F32 = jnp.float32
BF16 = jnp.bfloat16


def dp_index(y, x, c):
    return ((y % 2) * 4 + x % 4) * 2 + c % 2


def mp_index(y, z):
    return (y % 2) * 8 + z % 8


def dp_perm(target):
    return [
        (dp_index(y, x, c), dp_index(*target(y, x, c)))
        for y in range(2)
        for x in range(4)
        for c in range(2)
    ]


def mp_perm(target):
    return [(mp_index(y, z), mp_index(*target(y, z))) for y in range(2) for z in range(8)]


CORE = dp_perm(lambda y, x, c: (y, x, c + 1))
XUP = dp_perm(lambda y, x, c: (y, x + 1, c))
XDOWN = dp_perm(lambda y, x, c: (y, x - 1, c))
XPAIR = dp_perm(lambda y, x, c: (y, x ^ 1, c))
XFAR = dp_perm(lambda y, x, c: (y, x + 2, c))
YFAR = dp_perm(lambda y, x, c: (y + 1, x, c))
ZPAIR = mp_perm(lambda y, z: (y, z ^ 1))
ZFAR2 = mp_perm(lambda y, z: (y, z ^ 2))
ZFAR4 = mp_perm(lambda y, z: (y, z ^ 4))
YNEAR = mp_perm(lambda y, z: (y + 1, z))
ZUP = mp_perm(lambda y, z: (y, z + 1))
ZDOWN = mp_perm(lambda y, z: (y, z - 1))


def over_dp(values, perm):
    return lax.ppermute(values, "dp", perm)


def over_mp(values, perm):
    return lax.ppermute(values, "mp", perm)


def normalize(values, gain_row):
    row_mean = jnp.mean(values, axis=-1, keepdims=True)
    centred = values - row_mean
    variance = jnp.mean(centred * centred, axis=-1, keepdims=True)
    return centred * lax.rsqrt(variance + 1e-06) * gain_row


def sine_turns(turns):
    rest = turns - jnp.round(turns)
    square = rest * rest
    poly = SINE[4]
    for coefficient in SINE[3::-1]:
        poly = poly * square + coefficient
    return rest * (0.25 - square) * poly


def steps(col_peak, bit_count):
    levels = jnp.exp2(bit_count.astype(F32) - 1.0) - 1.0
    step_size = (col_peak.astype(F32) + 1e-06) / levels
    return jnp.stack([1.0 / step_size, step_size * (1.0 / (2.0 * math.pi))])


def call(body, grid, in_specs, out_specs, out_shape, flops, moved, prefetch=1, vmem_limit=VMEM_LIMIT):
    return pl.pallas_call(
        body,
        grid_spec=pltpu.PrefetchScalarGridSpec(
            num_scalar_prefetch=prefetch, grid=grid, in_specs=in_specs, out_specs=out_specs
        ),
        out_shape=out_shape,
        compiler_params=pltpu.CompilerParams(vmem_limit_bytes=vmem_limit),
        cost_estimate=COST,
    )


def whole(shape):
    return pl.BlockSpec(shape, lambda *_: (0,) * len(shape))


def lay_out(w_up, w_heads):
    depth, up_width = w_up.shape
    parts, part_width = w_heads.shape[1:]
    width = up_width + parts * part_width
    tile = 128

    def body(up_ref, heads_ref, raw_ref, peak_ref):
        raw_ref[:, :up_width] = up_ref[...]
        for part in range(parts):
            start = up_width + part * part_width
            raw_ref[:, start : start + part_width] = heads_ref[:, part, :]
        peak = jnp.max(jnp.abs(raw_ref[...].astype(F32)), axis=0, keepdims=True)

        @pl.when(pl.program_id(0) == 0)
        def _():
            peak_ref[...] = peak

        @pl.when(pl.program_id(0) > 0)
        def _():
            peak_ref[...] = jnp.maximum(peak_ref[...], peak)

    raw, peak = pl.pallas_call(
        body,
        grid=(depth // tile,),
        in_specs=[
            pl.BlockSpec((tile, up_width), lambda i: (i, 0)),
            pl.BlockSpec((tile, parts, part_width), lambda i: (i, 0, 0)),
        ],
        out_specs=[
            pl.BlockSpec((tile, width), lambda i: (i, 0)),
            pl.BlockSpec((1, width), lambda i: (0, 0)),
        ],
        out_shape=[
            jax.ShapeDtypeStruct((depth, width), BF16),
            jax.ShapeDtypeStruct((1, width), F32),
        ],
        compiler_params=pltpu.CompilerParams(vmem_limit_bytes=VMEM_LIMIT),
        cost_estimate=COST,
    )(w_up, w_heads)
    return raw, peak.reshape(width).astype(BF16)


def normalize_rows(tokens, gain, core, mp_place, total_rows):
    rows, width = tokens.shape
    count = width // SPAN // 2
    tile = 64
    own_blocks = width // lax.axis_size("mp") // BLK

    def body(place, tokens_ref, gain_ref, mine_ref, theirs_ref, gram_ref, full):
        value = normalize(tokens_ref[...].astype(F32), gain_ref[...]).astype(BF16)
        full[...] = value
        even = place[0] == 0

        @pl.when(even)
        def _():
            for j in range(count):
                mine_ref[j] = full[:, 2 * j * SPAN : (2 * j + 1) * SPAN]
                theirs_ref[j] = full[:, (2 * j + 1) * SPAN : (2 * j + 2) * SPAN]

        @pl.when(jnp.logical_not(even))
        def _():
            for j in range(count):
                theirs_ref[j] = full[:, 2 * j * SPAN : (2 * j + 1) * SPAN]
                mine_ref[j] = full[:, (2 * j + 1) * SPAN : (2 * j + 2) * SPAN]

        @pl.when(pl.program_id(0) == 0)
        def _():
            gram_ref[...] = jnp.zeros_like(gram_ref)

        for k in range(own_blocks):
            start = pl.multiple_of((place[1] * own_blocks + k) * BLK, BLK)
            columns = full[:, pl.ds(start, BLK)]
            gram_ref[k] += (
                lax.dot_general(columns, columns, (((0,), (0,)), ((), ())), preferred_element_type=F32)
                / total_rows
            )

    split = jax.ShapeDtypeStruct((count, rows, SPAN), BF16)
    return pl.pallas_call(
        body,
        grid_spec=pltpu.PrefetchScalarGridSpec(
            num_scalar_prefetch=1,
            grid=(rows // tile,),
            in_specs=[pl.BlockSpec((tile, width), lambda i, s: (i, 0)), whole((1, width))],
            out_specs=[
                pl.BlockSpec((count, tile, SPAN), lambda i, s: (0, i, 0)),
                pl.BlockSpec((count, tile, SPAN), lambda i, s: (0, i, 0)),
                whole((own_blocks, BLK, BLK)),
            ],
            scratch_shapes=[pltpu.VMEM((tile, width), BF16)],
        ),
        out_shape=[split, split, jax.ShapeDtypeStruct((own_blocks, BLK, BLK), F32)],
        compiler_params=pltpu.CompilerParams(vmem_limit_bytes=VMEM_LIMIT),
        cost_estimate=COST,
    )(jnp.stack([core, mp_place]), tokens, gain.reshape(1, -1))


def round_body(place, weight_ref, feed_ref, step_ref, out_ref):
    inverse, scale = step_ref[0:1, :], step_ref[1:2, :]
    for k in range(weight_ref.shape[0] // BLK):
        rows = slice(k * BLK, (k + 1) * BLK)
        value = weight_ref[rows, :].astype(F32)
        residual = (scale * sine_turns(value * inverse)).astype(BF16)
        value = value - jnp.dot(feed_ref[k], residual, preferred_element_type=F32)
        out_ref[rows, :] = (value - scale * sine_turns(value * inverse)).astype(BF16)


def round_weight(weight, feed, feed_place, step, tile):
    depth, width = weight.shape
    return call(
        round_body,
        (width // tile,),
        [
            pl.BlockSpec((depth, tile), lambda i, s: (0, i)),
            pl.BlockSpec((depth // BLK, BLK, BLK), lambda i, s: (s[0], 0, 0)),
            pl.BlockSpec((2, tile), lambda i, s: (0, i)),
        ],
        pl.BlockSpec((depth, tile), lambda i, s: (0, i)),
        jax.ShapeDtypeStruct((depth, width), BF16),
        45 * 128 * depth * width // 8,
        4 * depth * width,
    )(feed_place.reshape(1), weight, feed, step)


def round_merge(weight, feed, step, core):
    depth, width = weight.shape
    count = width // SPAN // 2

    def body(place, weight_ref, feed_ref, step_ref, out_ref):
        round_body(place, weight_ref, feed_ref, step_ref, out_ref.at[0])

    return call(
        body,
        (count,),
        [
            pl.BlockSpec((depth, SPAN), lambda i, s: (0, 2 * i + s[0])),
            whole(feed.shape),
            pl.BlockSpec((2, SPAN), lambda i, s: (0, 2 * i + s[0])),
        ],
        pl.BlockSpec((1, depth, SPAN), lambda i, s: (i, 0, 0)),
        jax.ShapeDtypeStruct((count, depth, SPAN), BF16),
        45 * 128 * depth * width // 16,
        2 * depth * width,
    )(core.reshape(1), weight, feed, step)


def multiply(mine, other, blocks, places, total=None, last=False):
    _, rows, _ = mine.shape
    count = len(blocks)
    width = blocks[0].shape[1]
    tile = 768

    def body(place, *refs):
        mine_refs, other_refs, block_refs = refs[:count], refs[count : 2 * count], refs[2 * count : 3 * count]
        refs = refs[3 * count :]
        value = None
        if total is not None:
            value, refs = refs[0][...], refs[1:]
        for first in range(0, count, 2):
            group = range(first, min(first + 2, count))
            left = jnp.concatenate(
                [
                    jnp.concatenate([row_refs[at][0] for at in group], axis=1)
                    for row_refs in (mine_refs, other_refs)
                ],
                axis=0,
            )
            right = jnp.concatenate([block_refs[at][...] for at in group], axis=0)
            piece = jnp.dot(left, right, preferred_element_type=F32)
            value = piece if value is None else value + piece
        if last:
            for part, ref in enumerate(refs):
                ref[...] = value[part * rows : (part + 1) * rows].astype(ref.dtype)
        else:
            refs[0][...] = value

    def row_spec(at):
        return pl.BlockSpec((1, rows, SPAN), lambda i, s: (s[at], 0, 0))

    both = pl.BlockSpec((2 * rows, tile), lambda i, s: (0, i))
    one = pl.BlockSpec((rows, tile), lambda i, s: (0, i))
    row_specs = [row_spec(at) for at in range(count)]
    operands = [mine] * count + [other] * count + list(blocks)
    in_specs = row_specs + row_specs + [pl.BlockSpec((SPAN, tile), lambda i, s: (0, i))] * count
    if total is not None:
        operands.append(total)
        in_specs.append(both)
    return call(
        body,
        (width // tile,),
        in_specs,
        [one, one] if last else both,
        [jax.ShapeDtypeStruct((rows, width), F32), jax.ShapeDtypeStruct((rows, width), BF16)]
        if last
        else jax.ShapeDtypeStruct((2 * rows, width), F32),
        4 * rows * SPAN * count * width,
        4 * rows * SPAN * count + 2 * SPAN * width * count + 8 * rows * width,
    )(jnp.stack(places), *operands)


def activate(mine, received, gains, keep, heads, total_rows):
    rows = mine.shape[0]
    head_width = heads * HD
    units = mine.shape[1] - 3 * head_width
    groups = units // BLK

    def body(mine_ref, received_ref, gain_ref, keep_ref, out_ref, gram_ref):
        def part(start, size):
            return mine_ref[:, start : start + size] + received_ref[:, start : start + size].astype(F32)

        for head in range(heads):
            start = head * HD
            query = normalize(part(units + start, HD), gain_ref[0:1, start : start + HD]).astype(BF16)
            keyed = normalize(part(units + head_width + start, HD), gain_ref[1:2, start : start + HD]).astype(BF16)
            value = part(units + 2 * head_width + start, HD).astype(BF16)
            scores = lax.dot_general(
                query, keyed, (((1,), (1,)), ((), ())), preferred_element_type=F32
            ) * (1.0 / math.sqrt(HD))
            weights = jnp.exp(scores - jnp.max(scores, axis=-1, keepdims=True))
            weights = (weights / jnp.sum(weights, axis=-1, keepdims=True)).astype(BF16)
            out_ref[:, start : start + HD] = jnp.dot(
                weights, value, preferred_element_type=F32
            ).astype(BF16)
        for group in range(groups):
            start = group * BLK
            unit = part(start, BLK)
            unit = 0.5 * unit * (1.0 + lax.erf(unit * math.sqrt(0.5)))
            unit = (unit * keep_ref[:, start : start + BLK]).astype(BF16)
            out_ref[:, head_width + start : head_width + start + BLK] = unit
            gram_ref[group] = (
                lax.dot_general(unit, unit, (((0,), (0,)), ((), ())), preferred_element_type=F32)
                / total_rows
            )

    return pl.pallas_call(
        body,
        out_shape=[
            jax.ShapeDtypeStruct((rows, head_width + units), BF16),
            jax.ShapeDtypeStruct((groups, BLK, BLK), F32),
        ],
        compiler_params=pltpu.CompilerParams(vmem_limit_bytes=VMEM_LIMIT),
        cost_estimate=COST,
    )(mine, received, gains, keep)


def project(acts, other_acts, merge, downs, merge_places, out_places):
    count = len(downs)
    rows = acts.shape[0]
    group = 2

    def body(place, acts_ref, other_ref, merge_ref, *refs):
        down_refs, outs = refs[:count], refs[count:]
        left = jnp.concatenate([acts_ref[...], other_ref[...]], axis=0)
        for first in range(0, count, group):
            right = jnp.concatenate(
                [
                    jnp.concatenate([merge_ref[place[at]], down_refs[at][...]], axis=0)
                    for at in range(first, first + group)
                ],
                axis=1,
            )
            value = jnp.dot(left, right, preferred_element_type=F32).astype(BF16)
            for part, out_ref in enumerate(outs):
                for at in range(group):
                    out_ref[place[count + first + at]] = value[
                        part * rows : (part + 1) * rows, at * SPAN : (at + 1) * SPAN
                    ]

    shape = (count, rows, SPAN)
    operands = [acts, other_acts, merge, *downs]
    return call(
        body,
        (1,),
        [whole(operand.shape) for operand in operands],
        [whole(shape), whole(shape)],
        [jax.ShapeDtypeStruct(shape, BF16)] * 2,
        4 * rows * acts.shape[1] * count * SPAN,
        2 * acts.shape[1] * count * SPAN + 8 * rows * count * SPAN,
        vmem_limit=56 * 2**20,
    )(jnp.stack([*merge_places, *out_places]), *operands)


def tied(*values):
    return lax.optimization_barrier(values)


def after(value, *others):
    return tied(value, *others)[0]


def shards(
    tokens,
    norm_gain,
    head_gains,
    w_heads,
    w_merge,
    w_up,
    w_down,
    feed_in,
    feed_merge,
    feed_down,
    layer_bits,
    hidden_keep,
):
    rows = tokens.shape[0]
    own = lax.axis_index("dp")
    y_pos, x_pos, core = own // 8, (own // 2) % 4, own % 2
    mp_place = lax.axis_index("mp")
    z_pos = mp_place % 8
    total_rows = rows * lax.axis_size("dp")
    keep_cols = jnp.repeat(hidden_keep.astype(F32), BLK).reshape(1, -1)

    def x_of(dx):
        return (x_pos + dx) % 4

    def place_of(dy, dx):
        return ((y_pos + dy) % 2) * 4 + x_of(dx)

    raw00, peak_in = lay_out(w_up, w_heads)
    peak_out = jnp.concatenate([jnp.max(jnp.abs(w_merge), axis=0), jnp.max(jnp.abs(w_down), axis=0)])

    def in_max(perm):
        return jnp.maximum(peak_in, over_dp(peak_in, perm))

    def out_max(perm):
        return jnp.maximum(peak_out, over_mp(peak_out, perm))

    peak_in, peak_out = tied(in_max(CORE), out_max(YNEAR))
    peak_in, peak_out = tied(in_max(XPAIR), out_max(ZPAIR))
    peak_in, raw00 = tied(in_max(XFAR), raw00)
    raw03, raw01 = over_dp(raw00, XUP), over_dp(raw00, XDOWN)
    peak_in, peak_out = tied(in_max(YFAR), out_max(ZFAR2))
    up_width, width = w_up.shape[1], w_merge.shape[1]
    step_in = jnp.concatenate(
        [steps(peak_in[:up_width], layer_bits[2]), steps(peak_in[up_width:], layer_bits[0])], axis=1
    )

    def rounded(block, dy, dx):
        return round_weight(block, feed_in, 2 * place_of(dy, dx) + core, step_in, 256)

    def rest(top, end):
        cut = top.shape[0] // 2
        return jnp.concatenate([over_dp(top[:cut], XUP), over_dp(end[cut:], XDOWN)], axis=0)

    q_in = {}
    q_in[0, 0] = rounded(raw00, 0, 0)
    q_in[1, 0] = over_dp(q_in[0, 0], YFAR)
    peak_out, _ = tied(out_max(ZFAR4), q_in[0, 0])
    step_merge = steps(peak_out[:width], layer_bits[1])
    step_down = steps(peak_out[width:], layer_bits[3])
    down00 = round_weight(w_down, feed_down, 0 * core, step_down, 128)
    down03, down01 = over_dp(down00, XUP), over_dp(down00, XDOWN)

    raw02 = rest(raw03, raw01)
    q_in[0, 3] = rounded(raw03, 0, 3)
    q_in[0, 1] = rounded(raw01, 0, 1)
    q_in[1, 3], q_in[1, 1] = over_dp(q_in[1, 0], XUP), over_dp(q_in[1, 0], XDOWN)
    down10 = over_dp(after(down00, q_in[1, 0]), YFAR)
    tokens, _ = tied(tokens, down00)
    mine, theirs, gram_in = normalize_rows(tokens, norm_gain, core, mp_place, total_rows)
    raw02, down10, down03, down01, theirs, _, _ = tied(
        raw02, down10, down03, down01, theirs, q_in[0, 3], q_in[0, 1]
    )
    q_in[0, 2] = rounded(raw02, 0, 2)
    q_in[1, 2] = over_dp(q_in[0, 2], YFAR)
    other = over_dp(theirs, CORE)
    down03, down01, w_merge, other, _ = tied(down03, down01, w_merge, other, q_in[0, 2])
    down02 = rest(down03, down01)
    q_merge = round_merge(w_merge, feed_merge, step_merge, core)

    def multiplied(keys, total=None, last=False):
        blocks, places = [q_in[k] for k in keys], [place_of(*k) for k in keys]
        return multiply(mine, other, blocks, places, total, last)

    total = multiplied(((0, 0), (1, 0), (0, 3), (0, 1)))
    down10, total, q_merge = tied(down10, total, q_merge)
    down13, down11 = over_dp(down10, XUP), over_dp(down10, XDOWN)
    total = multiplied(((0, 2), (1, 3), (1, 1)), total)
    down02, q_in[1, 2], total = tied(down02, q_in[1, 2], total)
    down12 = over_dp(down02, YFAR)
    kept, given = multiplied(((1, 2),), total, last=True)

    acts, gram_hidden = activate(
        kept, over_dp(given, CORE), head_gains, keep_cols, head_gains.shape[1] // HD, total_rows
    )
    acts_other = over_dp(acts, CORE)

    order = [(dy, dx) for dy in range(2) for dx in range(4)]
    downs = (down00, down01, down02, down03, down10, down11, down12, down13)
    places = [place_of(*key) for key in order]
    partial, others = project(acts, acts_other, q_merge, downs, places, places)
    swapped = over_dp(others, CORE)

    def chunk(offset):
        z_to = (z_pos + offset) % 8
        here = z_to % 2 == core
        return jnp.stack(
            [
                jnp.where(here, partial[y_to * 4 + z_to // 2], swapped[y_to * 4 + z_to // 2])
                for y_to in range(2)
            ]
        )

    def add(first, second):
        return (first.astype(F32) + second.astype(F32)).astype(BF16)

    cut = rows // 2
    far = chunk(4)
    up = over_mp(far[:, :cut], ZUP)
    down = over_mp(far[:, cut:], ZDOWN)
    base = chunk(3)
    up = over_mp(jnp.concatenate([add(base[:, :cut], up), base[:, cut:]], axis=1), ZUP)
    base = chunk(-3)
    down = over_mp(jnp.concatenate([base[:, :cut], add(base[:, cut:], down)], axis=1), ZDOWN)
    for hop in (2, 1):
        up = over_mp(add(chunk(hop), up), ZUP)
        down = over_mp(add(chunk(-hop), down), ZDOWN)
    summed = chunk(0).astype(F32) + up.astype(F32) + down.astype(F32)
    near = mp_place // 8 == 0
    keep_part = jnp.where(near, summed[0], summed[1])
    give_part = jnp.where(near, summed[1], summed[0]).astype(BF16)
    branch = (keep_part + over_mp(give_part, YNEAR).astype(F32)).astype(BF16)

    grams = jnp.concatenate([gram_in, gram_hidden], axis=0)
    for perm in (CORE, XPAIR, XFAR, YFAR):
        sent = grams.astype(BF16)
        grams = sent.astype(F32) + over_dp(sent, perm).astype(F32)
    in_count = gram_in.shape[0]
    return (branch, grams[:in_count], grams[in_count:])


def solution(mesh):
    in_specs = (
        P("dp", None),
        P(),
        P(None, "mp"),
        P("dp", None, "mp"),
        P("mp", None),
        P("dp", "mp"),
        P("mp", "dp"),
        P(),
        P("mp", None, None),
        P("mp", None, None),
        P(),
        P("mp"),
    )
    out_specs = (P("dp", "mp"), P("mp", None, None), P("mp", None, None))
    return jax.shard_map(shards, mesh=mesh, in_specs=in_specs, out_specs=out_specs, check_vma=False)
```
